32 devices in a mesh: ctx: 4 (over z), head: 8 (over y, x, core).
Axes of the slice: x: 2, y: 2, z: 4, core: 2. Of those that a mesh axis runs over, the one named last changes fastest.
Arguments:
- hyena_query: bfloat16 [2048, 8192], P('ctx', 'head'), may hold values from -6 to 6
- hyena_key: bfloat16 [2048, 8192], P('ctx', 'head'), may hold values from -6 to 6
- hyena_value: bfloat16 [2048, 8192], P('ctx', 'head'), may hold values from -6 to 6
- hyena_filter: bfloat16 [128, 8192], P(None, 'head'), may hold values from -0.5 to 0.5
- attn_query: bfloat16 [2048, 8192], P('ctx', 'head'), may hold values from -100 to 100
- attn_key: bfloat16 [2048, 8192], P('ctx', 'head'), may hold values from -4 to 4
- attn_value: bfloat16 [2048, 8192], P('ctx', 'head'), may hold values from -12 to 12
- segment_ids: int32 [2048], replicated, may hold values from 0 to 5, never falling along the last dimension, each value on 1 to 1024 neighbouring positions
- out_weight: bfloat16 [8192, 8192], P('head'), may hold values from -0.09375 to 0.09375
Outputs:
- hyena_out: bfloat16 [2048, 8192], P('ctx', 'head')
- stream: bfloat16 [2048, 8192], P('ctx', 'head')
The draws below stay inside these ranges and needn't reach their ends.
Inputs may be any that keep to these rules, and one draw needn't show every extreme that they name: `segment_ids`: never falls along the positions; each document is 1 to 1024 positions in a row, one exactly 1024.
All inputs are finite; a program needn't handle non-finite values.
Results may differ from the reference program's by a relative error of at most 0.014.
Values may be sent and summed in bfloat16 or wider, within the bound.
A program may use at most 320 MiB of HBM per device.

```python
import math
import jax
import jax.numpy as jnp
import numpy as np
from jax import lax

D = 8192
HEADS = 64
HEAD_DIM = 128
FILT = 128
SEGS = 6
LENGTH = 2048
N_HEAD = 8


def shared_pair(key):
    base_query = jax.random.truncated_normal(jax.random.fold_in(key, 11), -4.0, 4.0, (LENGTH, D), jnp.float32)
    base_key = jax.random.truncated_normal(jax.random.fold_in(key, 12), -4.0, 4.0, (LENGTH, D), jnp.float32)
    query_out = base_query
    key_out = base_key
    return (query_out, key_out)


def draw_attn_query(key, part):
    return shared_pair(key)[0].astype(jnp.bfloat16)


def draw_attn_key(key, part):
    return shared_pair(key)[1].astype(jnp.bfloat16)


def with_spikes(result, key, source, target, shards_of, factor):
    def block_of(axis_at):
        return (jnp.arange(result.shape[axis_at]) // (result.shape[axis_at] // shards_of)).reshape((-1,) + (1,) * (result.ndim - 1 - axis_at))

    first = jax.random.permutation(key, shards_of)[block_of(target)]
    far = (block_of(target) + shards_of // 2) % shards_of
    return jnp.where((block_of(source) == first) | (block_of(source) == far), factor * result, result)


def block_scale(stream_key, dims, cuts, least, high):
    gain = 1.0
    for axis_at, blocks in cuts:
        steps = jax.random.uniform(jax.random.fold_in(jax.random.fold_in(stream_key, 6), axis_at), (blocks,), jnp.float32, least / len(cuts), high / len(cuts))
        gain = gain * jnp.repeat(jnp.exp(steps), dims[axis_at] // blocks).reshape((-1,) + (1,) * (len(dims) - 1 - axis_at))
    return gain


def profile(number_of, total, bound, lean):
    portions = [(1 << 20) // math.isqrt(standing ** lean) + 1 for standing in range(2, number_of + 1)]
    rest, holding = total - bound - (number_of - 1), [1] * (number_of - 1)
    while rest > 0:
        free = [i for i in range(number_of - 1) if holding[i] < bound]
        whole, budget = sum([portions[i] for i in free]), rest
        for i in free:
            more = min(bound - holding[i], max(1, budget * portions[i] // whole), rest)
            holding[i] = holding[i] + more
            rest = rest - more
    return np.array([bound] + holding)


def ragged_sizes(stream_key, amount, total, most, lean):
    if amount == 2:
        one = jax.random.randint(stream_key, (), max(1, total - most), min(most, total - 1) + 1)
        return jnp.stack([one, total - one])
    tallies = jnp.asarray(profile(amount, total, most, lean), jnp.int32)
    couples = (amount - 1) // 2
    source_of, sink = tallies[1:1 + 2 * couples:2], tallies[2:2 + 2 * couples:2]
    room = jnp.minimum(source_of - 1, most - sink)
    moved = jax.random.randint(jax.random.fold_in(stream_key, 1), (couples,), 0, 1 << 20) % (room + 1)
    tallies = tallies.at[1:1 + 2 * couples:2].set(source_of - moved).at[2:2 + 2 * couples:2].set(sink + moved)
    return tallies[jax.random.permutation(jax.random.fold_in(stream_key, 2), amount)]


def normal_values(stream_key, extent, width, reach, pieces=(), kind=jnp.bfloat16):
    entries = jax.random.normal(stream_key, extent, jnp.float32) * width
    if len(pieces) > 0:
        entries = block_scale(stream_key, extent, pieces, -0.22, 0.18) * entries
    return jnp.clip(entries, min=-reach, max=reach).astype(kind)


def noise_with(key, shape, width, most, cuts, heavy, kind=jnp.bfloat16):
    values = width * jax.random.normal(key, shape, jnp.float32)
    if cuts:
        values = values * block_scale(key, shape, cuts, -0.22, 0.18)
    return jnp.clip(with_spikes(values, jax.random.fold_in(key, 3), *heavy), -most, most).astype(kind)


def setup_inputs(seed: int = 0) -> dict:
    key_list = jax.random.split(jax.random.key(seed), 10)
    return {
        "hyena_query": normal_values(key_list[0], (LENGTH, D), 1.0, 6.0, ((0, 4), (1, 8))),
        "hyena_key": normal_values(key_list[1], (LENGTH, D), 1.0, 6.0, ((0, 4), (1, 8))),
        "hyena_value": normal_values(key_list[2], (LENGTH, D), 1.0, 6.0, ((0, 4), (1, 8))),
        "hyena_filter": normal_values(key_list[3], (FILT, D), FILT ** -0.5, 0.5, ((1, 8),)),
        "attn_query": draw_attn_query(jax.random.fold_in(key_list[9], 71), 0),
        "attn_key": draw_attn_key(jax.random.fold_in(key_list[9], 71), 0),
        "attn_value": normal_values(key_list[6], (LENGTH, D), 2.0, 12.0, ((0, 4), (1, 8))),
        "segment_ids": jnp.searchsorted(jnp.cumsum(ragged_sizes(key_list[7], SEGS, LENGTH, LENGTH // 2, 0)), jnp.arange(LENGTH), side="right").astype(jnp.int32),
        "out_weight": noise_with(key_list[8], (D, D), D ** -0.5, 0.09375, ((0, 8),), (0, 1, 8, 2.0)),
    }


def hyena_mix(hyena_query, hyena_key, hyena_value, hyena_filter):
    signal = lax.optimization_barrier((hyena_key.astype(jnp.float32) * hyena_value.astype(jnp.float32)).astype(jnp.bfloat16)).astype(jnp.float32)
    padded = jnp.pad(signal, ((FILT, 0), (0, 0)))
    filter_taps = hyena_filter.astype(jnp.float32)

    def add_tap(tap_index, filtered):
        tap_row = lax.dynamic_index_in_dim(filter_taps, tap_index, 0, keepdims=True)
        moved = lax.dynamic_slice_in_dim(padded, (FILT - tap_index).astype(jnp.int32), LENGTH, 0)
        return filtered + tap_row * moved

    filtered = lax.fori_loop(jnp.int32(0), jnp.int32(FILT), add_tap, jnp.zeros((LENGTH, D), jnp.float32))
    return (hyena_query.astype(jnp.float32) * filtered).astype(jnp.bfloat16)


def reference(hyena_query, hyena_key, hyena_value, hyena_filter, attn_query, attn_key, attn_value, segment_ids, out_weight):
    hyena_out = hyena_mix(hyena_query, hyena_key, hyena_value, hyena_filter)
    positions = jnp.arange(LENGTH, dtype=jnp.int32)
    allowed = (positions[None, :] <= positions[:, None]) & (segment_ids[None, :] == segment_ids[:, None])
    score_scale = HEAD_DIM ** -0.5

    def one_head(head_index):
        first_col = (head_index * HEAD_DIM).astype(jnp.int32)
        query_head = lax.dynamic_slice_in_dim(attn_query, first_col, HEAD_DIM, 1)
        key_head = lax.dynamic_slice_in_dim(attn_key, first_col, HEAD_DIM, 1)
        value_head = lax.dynamic_slice_in_dim(attn_value, first_col, HEAD_DIM, 1)
        scores = jnp.dot(query_head, key_head.T, preferred_element_type=jnp.float32) * score_scale
        row_top = jnp.max(jnp.where(allowed, scores, -1e30), axis=1)
        probs = jnp.where(allowed, jnp.exp(scores - row_top[:, None]), 0.0)
        row_total = jnp.sum(probs, axis=1)
        weighted = jnp.dot(probs.astype(jnp.bfloat16), value_head, preferred_element_type=jnp.float32)
        return (weighted / row_total[:, None]).astype(jnp.bfloat16)

    head_outputs = lax.map(one_head, jnp.arange(HEADS, dtype=jnp.int32))
    attended = jnp.transpose(head_outputs, (1, 0, 2)).reshape(LENGTH, D)
    group_width = D // N_HEAD

    def add_group(group_index, total):
        first_col = (group_index * group_width).astype(jnp.int32)
        columns = lax.dynamic_slice_in_dim(attended, first_col, group_width, 1)
        rows = lax.dynamic_slice_in_dim(out_weight, first_col, group_width, 0)
        term = jnp.dot(columns, rows, preferred_element_type=jnp.float32).astype(jnp.bfloat16)
        return total + term.astype(jnp.float32)

    projected = lax.fori_loop(jnp.int32(0), jnp.int32(N_HEAD), add_group, jnp.zeros((LENGTH, D), jnp.float32))
    stream = (hyena_out.astype(jnp.float32) + projected).astype(jnp.bfloat16)
    return (hyena_out, stream)
```

```python
import functools

import jax
import jax.numpy as jnp
import numpy as np
from jax import lax
from jax.experimental import pallas as pl
from jax.experimental.pallas import tpu as pltpu
from jax.sharding import PartitionSpec as P

HEAD_DIM = 128
LOG2_E = 1.4426950408889634
QUERY_TILE = 256
CHANNEL_TILE = 256


def shifted(x, axis, by):
    devices = lax.axis_size(axis)
    pairs = [(i, i + by) for i in range(devices) if 0 <= i + by < devices]
    return lax.ppermute(x, axis, pairs)


def split_high_low(matrix):
    exact = jnp.asarray(matrix, jnp.float32)
    high = exact.astype(jnp.bfloat16)
    low = (exact - high.astype(jnp.float32)).astype(jnp.bfloat16)
    return high, low


def fourier_matrices(taps):
    size = 2 * taps
    n = np.arange(size)
    k = np.arange(taps)
    angle = 2.0 * np.pi * np.outer(k, n) / size
    alternating = np.where(n % 2 == 0, 1.0, -1.0)
    forward = np.concatenate([np.cos(angle), alternating[None], np.sin(angle)[1:]], axis=0)
    gain = np.full((size,), 2.0 / size)
    gain[0] = gain[taps] = 1.0 / size
    inverse = (forward * gain[:, None]).T[taps:]
    return forward.astype(np.float32), inverse.astype(np.float32)


def dot32(a, b):
    return jnp.dot(a, b, preferred_element_type=jnp.float32)


def hyena_kernel(rim_ref, query_ref, key_ref, value_ref, taps_ref, fh_ref, fl_ref, gh_ref, gl_ref, out_ref):
    rows, _ = key_ref.shape
    taps = taps_ref.shape[0]
    fh, fl, gh, gl = fh_ref[...], fl_ref[...], gh_ref[...], gl_ref[...]
    tap_freq = dot32(fh[:, :taps], taps_ref[...]) + dot32(fl[:, :taps], taps_ref[...])
    tap_cos, tap_sin = tap_freq[:taps], tap_freq[taps:]
    edge = lax.broadcasted_iota(jnp.int32, tap_cos.shape, 0) == 0
    before = rim_ref[...]
    for block in range(rows // taps):
        here = slice(block * taps, (block + 1) * taps)
        now = (key_ref[here, :].astype(jnp.float32) * value_ref[here, :].astype(jnp.float32)).astype(jnp.bfloat16)
        window = jnp.concatenate([before, now], axis=0)
        freq = dot32(fh, window) + dot32(fl, window)
        cos, sin = freq[:taps], freq[taps:]
        sin_sin = sin * tap_sin
        real = cos * tap_cos - jnp.where(edge, 0.0, sin_sin)
        imag = jnp.where(edge, sin_sin, cos * tap_sin + sin * tap_cos)
        product = jnp.concatenate([real, imag], axis=0)
        high = product.astype(jnp.bfloat16)
        low = (product - high.astype(jnp.float32)).astype(jnp.bfloat16)
        filtered = dot32(gh, high) + dot32(gh, low) + dot32(gl, high)
        out_ref[here, :] = (query_ref[here, :].astype(jnp.float32) * filtered).astype(jnp.bfloat16)
        before = now


def hyena(rim, query, key, value, taps):
    rows, width = key.shape
    tap_count = taps.shape[0]
    forward, inverse = fourier_matrices(tap_count)
    constants = split_high_low(forward) + split_high_low(inverse)
    column = lambda r: pl.BlockSpec((r, CHANNEL_TILE), lambda i: (0, i))
    whole = lambda a: pl.BlockSpec(a.shape, lambda i: (0, 0))
    return pl.pallas_call(
        hyena_kernel,
        out_shape=jax.ShapeDtypeStruct((rows, width), jnp.bfloat16),
        grid=(width // CHANNEL_TILE,),
        in_specs=[column(tap_count), column(rows), column(rows), column(rows), column(tap_count)]
        + [whole(a) for a in constants],
        out_specs=column(rows),
        compiler_params=pltpu.CompilerParams(vmem_limit_bytes=48 * 2**20),
        cost_estimate=pl.CostEstimate(flops=3 * 10**9, bytes_accessed=5 * 2**20, transcendentals=0),
    )(rim, query, key, value, taps, *constants)


def attention_kernel(hops, start_ref, query_ref, *refs):
    key_refs, value_refs, out_ref = refs[: hops + 1], refs[hops + 1 : 2 * hops + 2], refs[-1]
    rows = query_ref.shape[0]
    scale = HEAD_DIM ** (-0.5) * LOG2_E
    for tile in range(rows // QUERY_TILE):
        low, high = tile * QUERY_TILE, (tile + 1) * QUERY_TILE
        query = query_ref[low:high, :]
        start = start_ref[low:high, :]
        parts = []
        for back in range(hops, -1, -1):
            first = low if back == hops else 0
            last = high if back == 0 else rows
            scores = lax.dot_general(
                query, key_refs[back][first:last, :], (((1,), (1,)), ((), ())), preferred_element_type=jnp.float32
            )
            position = lax.broadcasted_iota(jnp.int32, scores.shape, 1) + (first - back * rows)
            allowed = position >= start
            if back == 0:
                allowed &= position <= lax.broadcasted_iota(jnp.int32, scores.shape, 0) + low
            parts.append((back, first, last, jnp.where(allowed, scores, -1e30)))
        top = functools.reduce(jnp.maximum, [jnp.max(part[3], axis=1, keepdims=True) for part in parts])
        total = jnp.zeros((QUERY_TILE, 1), jnp.float32)
        weighted = jnp.zeros((QUERY_TILE, HEAD_DIM), jnp.float32)
        for back, first, last, scores in parts:
            probs = jnp.exp2((scores - top) * scale)
            total += jnp.sum(probs, axis=1, keepdims=True)
            weighted += dot32(probs.astype(jnp.bfloat16), value_refs[back][first:last, :])
        out_ref[low:high, :] = (weighted / total).astype(jnp.bfloat16)


def attention(start, query, keys, values):
    rows, width = query.shape
    hops = len(keys) - 1
    head = pl.BlockSpec((rows, HEAD_DIM), lambda h: (0, h))
    return pl.pallas_call(
        functools.partial(attention_kernel, hops),
        out_shape=jax.ShapeDtypeStruct((rows, width), jnp.bfloat16),
        grid=(width // HEAD_DIM,),
        in_specs=[pl.BlockSpec((rows, 1), lambda h: (0, 0)), head] + [head] * (2 * hops + 2),
        out_specs=head,
        compiler_params=pltpu.CompilerParams(vmem_limit_bytes=48 * 2**20),
        cost_estimate=pl.CostEstimate(flops=4 * 10**9, bytes_accessed=8 * 2**20, transcendentals=6 * 10**6),
    )(start, query, *keys, *values)


def on_device(
    hyena_query,
    hyena_key,
    hyena_value,
    hyena_filter,
    attn_query,
    attn_key,
    attn_value,
    segment_ids,
    out_weight,
):
    num_rows = hyena_key.shape[0]
    tap_count = hyena_filter.shape[0]
    hops = lax.axis_size("ctx") // 2
    last_key = hyena_key[num_rows - tap_count :].astype(jnp.float32)
    last_value = hyena_value[num_rows - tap_count :].astype(jnp.float32)
    rim = shifted((last_key * last_value).astype(jnp.bfloat16), "ctx", 1)
    keys, values = [attn_key], [attn_value]
    for _ in range(hops):
        keys.append(shifted(keys[-1], "ctx", 1))
        values.append(shifted(values[-1], "ctx", 1))
    hyena_out = hyena(rim, hyena_query, hyena_key, hyena_value, hyena_filter)
    offset = lax.axis_index("ctx") * num_rows
    own_segments = lax.dynamic_slice_in_dim(segment_ids, offset, num_rows)
    document_start = jnp.sum((segment_ids[None, :] < own_segments[:, None]).astype(jnp.int32), axis=1)
    start = (document_start - offset)[:, None]
    attended = attention(start, attn_query, keys, values)
    partial_terms = jnp.dot(attended, out_weight, preferred_element_type=jnp.float32)
    projected = lax.psum_scatter(
        partial_terms.astype(jnp.bfloat16), "head", scatter_dimension=1, tiled=True
    ).astype(jnp.float32)
    stream = (hyena_out.astype(jnp.float32) + projected).astype(jnp.bfloat16)
    return (hyena_out, stream)


def solution(mesh):
    return jax.shard_map(
        on_device,
        mesh=mesh,
        in_specs=(
            P("ctx", "head"),
            P("ctx", "head"),
            P("ctx", "head"),
            P(None, "head"),
            P("ctx", "head"),
            P("ctx", "head"),
            P("ctx", "head"),
            P(),
            P("head", None),
        ),
        out_specs=(P("ctx", "head"), P("ctx", "head")),
        check_vma=False,
    )
```

```python
import functools

import jax
import jax.numpy as jnp
import numpy as np
from jax import lax
from jax.experimental import pallas as pl
from jax.experimental.pallas import tpu as pltpu
from jax.sharding import PartitionSpec as P

HEAD_DIM = 128
LOG2_E = 1.4426950408889634
QUERY_TILE = 256
CHANNEL_TILE = 256
PROJECT_ROWS = 128
MESH = pl.DeviceIdType.MESH


def shifted(x, axis, by):
    devices = lax.axis_size(axis)
    pairs = [(i, i + by) for i in range(devices) if 0 <= i + by < devices]
    return lax.ppermute(x, axis, pairs)


def split_high_low(matrix):
    exact = jnp.asarray(matrix, jnp.float32)
    high = exact.astype(jnp.bfloat16)
    low = (exact - high.astype(jnp.float32)).astype(jnp.bfloat16)
    return high, low


def fourier_matrices(taps):
    size = 2 * taps
    n = np.arange(size)
    k = np.arange(taps)
    angle = 2.0 * np.pi * np.outer(k, n) / size
    alternating = np.where(n % 2 == 0, 1.0, -1.0)
    forward = np.concatenate([np.cos(angle), alternating[None], np.sin(angle)[1:]], axis=0)
    gain = np.full((size,), 2.0 / size)
    gain[0] = gain[taps] = 1.0 / size
    inverse = (forward * gain[:, None]).T[taps:]
    return forward.astype(np.float32), inverse.astype(np.float32)


def dot32(a, b):
    return jnp.dot(a, b, preferred_element_type=jnp.float32)


def hyena_kernel(rim_ref, query_ref, key_ref, value_ref, taps_ref, fh_ref, fl_ref, gh_ref, gl_ref, out_ref):
    rows, _ = key_ref.shape
    taps = taps_ref.shape[0]
    fh, fl, gh, gl = fh_ref[...], fl_ref[...], gh_ref[...], gl_ref[...]
    tap_freq = dot32(fh[:, :taps], taps_ref[...]) + dot32(fl[:, :taps], taps_ref[...])
    tap_cos, tap_sin = tap_freq[:taps], tap_freq[taps:]
    edge = lax.broadcasted_iota(jnp.int32, tap_cos.shape, 0) == 0
    before = rim_ref[...]
    for block in range(rows // taps):
        here = slice(block * taps, (block + 1) * taps)
        now = (key_ref[here, :].astype(jnp.float32) * value_ref[here, :].astype(jnp.float32)).astype(jnp.bfloat16)
        window = jnp.concatenate([before, now], axis=0)
        freq = dot32(fh, window) + dot32(fl, window)
        cos, sin = freq[:taps], freq[taps:]
        sin_sin = sin * tap_sin
        real = cos * tap_cos - jnp.where(edge, 0.0, sin_sin)
        imag = jnp.where(edge, sin_sin, cos * tap_sin + sin * tap_cos)
        product = jnp.concatenate([real, imag], axis=0)
        high = product.astype(jnp.bfloat16)
        low = (product - high.astype(jnp.float32)).astype(jnp.bfloat16)
        filtered = dot32(gh, high) + dot32(gh, low) + dot32(gl, high)
        out_ref[here, :] = (query_ref[here, :].astype(jnp.float32) * filtered).astype(jnp.bfloat16)
        before = now


def hyena(rim, query, key, value, taps):
    rows, width = key.shape
    tap_count = taps.shape[0]
    forward, inverse = fourier_matrices(tap_count)
    constants = split_high_low(forward) + split_high_low(inverse)
    column = lambda r: pl.BlockSpec((r, CHANNEL_TILE), lambda i: (0, i))
    whole = lambda a: pl.BlockSpec(a.shape, lambda i: (0, 0))
    return pl.pallas_call(
        hyena_kernel,
        out_shape=jax.ShapeDtypeStruct((rows, width), jnp.bfloat16),
        grid=(width // CHANNEL_TILE,),
        in_specs=[column(tap_count), column(rows), column(rows), column(rows), column(tap_count)]
        + [whole(a) for a in constants],
        out_specs=column(rows),
        compiler_params=pltpu.CompilerParams(vmem_limit_bytes=48 * 2**20),
        cost_estimate=pl.CostEstimate(flops=3 * 10**9, bytes_accessed=5 * 2**20, transcendentals=0),
    )(rim, query, key, value, taps, *constants)


def attention_kernel(hops, start_ref, query_ref, *refs):
    key_refs, value_refs, out_ref = refs[: hops + 1], refs[hops + 1 : 2 * hops + 2], refs[-1]
    rows = query_ref.shape[0]
    scale = HEAD_DIM ** (-0.5) * LOG2_E
    for tile in range(rows // QUERY_TILE):
        low, high = tile * QUERY_TILE, (tile + 1) * QUERY_TILE
        query = query_ref[low:high, :]
        start = start_ref[low:high, :]
        parts = []
        for back in range(hops, -1, -1):
            first = low if back == hops else 0
            last = high if back == 0 else rows
            scores = lax.dot_general(
                query, key_refs[back][first:last, :], (((1,), (1,)), ((), ())), preferred_element_type=jnp.float32
            )
            position = lax.broadcasted_iota(jnp.int32, scores.shape, 1) + (first - back * rows)
            allowed = position >= start
            if back == 0:
                allowed &= position <= lax.broadcasted_iota(jnp.int32, scores.shape, 0) + low
            parts.append((back, first, last, jnp.where(allowed, scores, -1e30)))
        top = functools.reduce(jnp.maximum, [jnp.max(part[3], axis=1, keepdims=True) for part in parts])
        total = jnp.zeros((QUERY_TILE, 1), jnp.float32)
        weighted = jnp.zeros((QUERY_TILE, HEAD_DIM), jnp.float32)
        for back, first, last, scores in parts:
            probs = jnp.exp2((scores - top) * scale)
            total += jnp.sum(probs, axis=1, keepdims=True)
            weighted += dot32(probs.astype(jnp.bfloat16), value_refs[back][first:last, :])
        out_ref[low:high, :] = (weighted / total).astype(jnp.bfloat16)


def attention(start, query, keys, values):
    rows, width = query.shape
    hops = len(keys) - 1
    head = pl.BlockSpec((rows, HEAD_DIM), lambda h: (0, h))
    return pl.pallas_call(
        functools.partial(attention_kernel, hops),
        out_shape=jax.ShapeDtypeStruct((rows, width), jnp.bfloat16),
        grid=(width // HEAD_DIM,),
        in_specs=[pl.BlockSpec((rows, 1), lambda h: (0, 0)), head] + [head] * (2 * hops + 2),
        out_specs=head,
        compiler_params=pltpu.CompilerParams(vmem_limit_bytes=48 * 2**20),
        cost_estimate=pl.CostEstimate(flops=4 * 10**9, bytes_accessed=8 * 2**20, transcendentals=6 * 10**6),
    )(start, query, *keys, *values)


def project_kernel(n, chunk, attended_ref, hyena_ref, weight_ref, out_ref, weights, away, near, landed, load_sem, send_sem, recv_sem):
    rows, width = out_ref.shape
    chunks = rows // chunk
    stages = n.bit_length() - 1
    me = lax.axis_index("head")
    core = me % 2

    def flip(bit, by):
        return bit + by - 2 * bit * by

    def slot_bit(slot, stage):
        return (slot // (n >> (stage + 1))) % 2

    def destination(slot):
        to_core = flip(core, slot_bit(slot, 0))
        place = to_core
        for axis in range(1, stages):
            across = slot_bit(slot, axis) * (1 - to_core) + slot_bit(slot, stages - axis) * to_core
            place = place + flip((me // 2**axis) % 2, across) * 2**axis
        return place

    def partner(stage):
        if stage == 0:
            return me + 1 - 2 * core
        forward = me + (1 - 2 * ((me // 2**stage) % 2)) * 2**stage
        other = stages - stage
        backward = me + (1 - 2 * ((me // 2**other) % 2)) * 2**other
        return forward * (1 - core) + backward * core

    loads = []
    for slot in list(range(n // 2, n)) + list(range(n // 2)):
        columns = pl.ds(pl.multiple_of(destination(slot) * width, width), width)
        load = pltpu.make_async_copy(weight_ref.at[:, columns], weights.at[slot], load_sem.at[slot])
        load.start()
        loads.append((slot, load))

    barrier = pltpu.get_barrier_semaphore()
    for stage in range(stages):
        pl.semaphore_signal(barrier, inc=1, device_id={"head": partner(stage)}, device_id_type=MESH)
    pl.semaphore_wait(barrier, stages)

    first_of = [n - (n >> stage) for stage in range(stages)]

    def copy(stage, part):
        count = n >> (stage + 1)
        source = away.at[part] if stage == 0 else near.at[part, pl.ds(count, count)]
        return pltpu.make_async_remote_copy(
            src_ref=source,
            dst_ref=landed.at[part, pl.ds(first_of[stage], count)],
            send_sem=send_sem.at[stage, part],
            recv_sem=recv_sem.at[stage, part],
            device_id={"head": partner(stage)},
            device_id_type=MESH,
        )

    def term(part, slot):
        return jnp.dot(
            attended_ref[part * chunk : (part + 1) * chunk, :], weights[slot], preferred_element_type=jnp.float32
        )

    def far_terms(part):
        if part == 0:
            for _, load in loads[: n // 2]:
                load.wait()

        @pl.loop(0, n // 2)
        def _(index):
            away[part, index] = term(part, index + n // 2).astype(jnp.bfloat16)

        copy(0, part).start()

    def near_terms(part):
        if part == 0:
            for _, load in loads[n // 2 :]:
                load.wait()
        copy(0, part).wait_recv()

        def add(index):
            total = term(part, index) + landed[part, index].astype(jnp.float32)
            near[part, index] = total.astype(jnp.bfloat16)

        pl.loop(n // 4, n // 2)(add)
        copy(1, part).start()
        pl.loop(0, n // 4)(add)

    def fold(stage, part):
        copy(stage, part).wait_recv()
        half = n >> (stage + 2)

        def add(index):
            arrived = landed[part, first_of[stage] + index].astype(jnp.float32)
            near[part, index] = (near[part, index].astype(jnp.float32) + arrived).astype(jnp.bfloat16)

        pl.loop(half, 2 * half)(add)
        copy(stage + 1, part).start()
        pl.loop(0, half)(add)

    def finish(part):
        last = stages - 1
        copy(last, part).wait_recv()
        here = slice(part * chunk, (part + 1) * chunk)
        total = near[part, 0].astype(jnp.float32) + landed[part, first_of[last]].astype(jnp.float32)
        out_ref[here, :] = (hyena_ref[here, :].astype(jnp.float32) + total).astype(jnp.bfloat16)

    for step in range(chunks + stages):
        if step < chunks:
            far_terms(step)
        for stage in range(1, stages):
            if 0 <= step - stage < chunks:
                near_terms(step - 1) if stage == 1 else fold(stage - 1, step - stage)
        if 0 <= step - stages < chunks:
            finish(step - stages)
    for stage in range(stages):
        for part in range(chunks):
            copy(stage, part).wait_send()


def project(attended, hyena_out, weight):
    rows, width = attended.shape
    n = lax.axis_size("head")
    chunks = rows // PROJECT_ROWS
    stages = n.bit_length() - 1
    vmem = pl.BlockSpec(memory_space=pltpu.VMEM)
    return pl.pallas_call(
        functools.partial(project_kernel, n, PROJECT_ROWS),
        out_shape=jax.ShapeDtypeStruct((rows, width), jnp.bfloat16),
        in_specs=[vmem, vmem, pl.BlockSpec(memory_space=pl.ANY)],
        out_specs=vmem,
        scratch_shapes=[
            pltpu.VMEM((n, width, width), jnp.bfloat16),
            pltpu.VMEM((chunks, n // 2, PROJECT_ROWS, width), jnp.bfloat16),
            pltpu.VMEM((chunks, n // 2, PROJECT_ROWS, width), jnp.bfloat16),
            pltpu.VMEM((chunks, n - 1, PROJECT_ROWS, width), jnp.bfloat16),
            pltpu.SemaphoreType.DMA((n,)),
            pltpu.SemaphoreType.DMA((stages, chunks)),
            pltpu.SemaphoreType.DMA((stages, chunks)),
        ],
        compiler_params=pltpu.CompilerParams(
            collective_id=0, has_side_effects=True, vmem_limit_bytes=56 * 2**20
        ),
        cost_estimate=pl.CostEstimate(flops=9 * 10**9, bytes_accessed=20 * 2**20, transcendentals=0),
    )(attended, hyena_out, weight)


def on_device(
    hyena_query,
    hyena_key,
    hyena_value,
    hyena_filter,
    attn_query,
    attn_key,
    attn_value,
    segment_ids,
    out_weight,
):
    num_rows = hyena_key.shape[0]
    tap_count = hyena_filter.shape[0]
    hops = lax.axis_size("ctx") // 2
    last_key = hyena_key[num_rows - tap_count :].astype(jnp.float32)
    last_value = hyena_value[num_rows - tap_count :].astype(jnp.float32)
    rim = shifted((last_key * last_value).astype(jnp.bfloat16), "ctx", 1)
    keys, values = [attn_key], [attn_value]
    for _ in range(hops):
        keys.append(shifted(keys[-1], "ctx", 1))
        values.append(shifted(values[-1], "ctx", 1))
    hyena_out = hyena(rim, hyena_query, hyena_key, hyena_value, hyena_filter)
    offset = lax.axis_index("ctx") * num_rows
    own_segments = lax.dynamic_slice_in_dim(segment_ids, offset, num_rows)
    document_start = jnp.sum((segment_ids[None, :] < own_segments[:, None]).astype(jnp.int32), axis=1)
    start = (document_start - offset)[:, None]
    start, hyena_out = lax.optimization_barrier((start, hyena_out))
    attended = attention(start, attn_query, keys, values)
    stream = project(attended, hyena_out, out_weight)
    return (hyena_out, stream)


def solution(mesh):
    return jax.shard_map(
        on_device,
        mesh=mesh,
        in_specs=(
            P("ctx", "head"),
            P("ctx", "head"),
            P("ctx", "head"),
            P(None, "head"),
            P("ctx", "head"),
            P("ctx", "head"),
            P("ctx", "head"),
            P(),
            P("head", None),
        ),
        out_specs=(P("ctx", "head"), P("ctx", "head")),
        check_vma=False,
    )
```

```python
import functools

import jax
import jax.numpy as jnp
import numpy as np
from jax import lax
from jax.experimental import pallas as pl
from jax.experimental.pallas import tpu as pltpu
from jax.sharding import PartitionSpec as P

HEAD_DIM = 128
LOG2_E = 1.4426950408889634
CHANNEL_TILE = 256
MIX_ROWS = 128
MESH = pl.DeviceIdType.MESH


def shifted(x, axis, by):
    devices = lax.axis_size(axis)
    pairs = [(i, i + by) for i in range(devices) if 0 <= i + by < devices]
    return lax.ppermute(x, axis, pairs)


def split_high_low(matrix):
    exact = jnp.asarray(matrix, jnp.float32)
    high = exact.astype(jnp.bfloat16)
    low = (exact - high.astype(jnp.float32)).astype(jnp.bfloat16)
    return high, low


def fourier_matrices(taps):
    size = 2 * taps
    n = np.arange(size)
    k = np.arange(taps)
    angle = 2.0 * np.pi * np.outer(k, n) / size
    alternating = np.where(n % 2 == 0, 1.0, -1.0)
    forward = np.concatenate([np.cos(angle), alternating[None], np.sin(angle)[1:]], axis=0)
    gain = np.full((size,), 2.0 / size)
    gain[0] = gain[taps] = 1.0 / size
    inverse = (forward * gain[:, None]).T[taps:]
    return forward.astype(np.float32), inverse.astype(np.float32)


def dot32(a, b):
    return jnp.dot(a, b, preferred_element_type=jnp.float32)


def hyena_kernel(
    rim_ref, query_ref, key_ref, value_ref, taps_ref, projected_ref, fh_ref, fl_ref, gh_ref, gl_ref, out_ref, stream_ref
):
    rows, _ = key_ref.shape
    taps = taps_ref.shape[0]
    fh, fl, gh, gl = fh_ref[...], fl_ref[...], gh_ref[...], gl_ref[...]
    tap_freq = dot32(fh[:, :taps], taps_ref[...]) + dot32(fl[:, :taps], taps_ref[...])
    tap_cos, tap_sin = tap_freq[:taps], tap_freq[taps:]
    edge = lax.broadcasted_iota(jnp.int32, tap_cos.shape, 0) == 0
    before = rim_ref[...]
    for block in range(rows // taps):
        here = slice(block * taps, (block + 1) * taps)
        now = (key_ref[here, :].astype(jnp.float32) * value_ref[here, :].astype(jnp.float32)).astype(jnp.bfloat16)
        window = jnp.concatenate([before, now], axis=0)
        freq = dot32(fh, window) + dot32(fl, window)
        cos, sin = freq[:taps], freq[taps:]
        sin_sin = sin * tap_sin
        real = cos * tap_cos - jnp.where(edge, 0.0, sin_sin)
        imag = jnp.where(edge, sin_sin, cos * tap_sin + sin * tap_cos)
        product = jnp.concatenate([real, imag], axis=0)
        high = product.astype(jnp.bfloat16)
        low = (product - high.astype(jnp.float32)).astype(jnp.bfloat16)
        filtered = dot32(gh, high) + dot32(gh, low) + dot32(gl, high)
        hyena_out = (query_ref[here, :].astype(jnp.float32) * filtered).astype(jnp.bfloat16)
        out_ref[here, :] = hyena_out
        stream_ref[here, :] = (hyena_out.astype(jnp.float32) + projected_ref[here, :]).astype(jnp.bfloat16)
        before = now


def hyena(rim, query, key, value, taps, projected):
    rows, width = key.shape
    tap_count = taps.shape[0]
    forward, inverse = fourier_matrices(tap_count)
    constants = split_high_low(forward) + split_high_low(inverse)
    column = lambda r: pl.BlockSpec((r, CHANNEL_TILE), lambda i: (0, i))
    whole = lambda a: pl.BlockSpec(a.shape, lambda i: (0, 0))
    return pl.pallas_call(
        hyena_kernel,
        out_shape=[jax.ShapeDtypeStruct((rows, width), jnp.bfloat16)] * 2,
        grid=(width // CHANNEL_TILE,),
        in_specs=[column(tap_count), column(rows), column(rows), column(rows), column(tap_count), column(rows)]
        + [whole(a) for a in constants],
        out_specs=[column(rows)] * 2,
        compiler_params=pltpu.CompilerParams(vmem_limit_bytes=48 * 2**20),
        cost_estimate=pl.CostEstimate(flops=3 * 10**9, bytes_accessed=5 * 2**20, transcendentals=0),
    )(rim, query, key, value, taps, projected, *constants)


def spread_exactly(value, lane, head, heads, into):
    high = value.astype(jnp.bfloat16).astype(jnp.float32)
    middle = (value - high).astype(jnp.bfloat16).astype(jnp.float32)
    low = value - high - middle
    into = jnp.where(lane == head, high, into)
    into = jnp.where(lane == head + heads, middle, into)
    return jnp.where(lane == head + 2 * heads, low, into)


def gathered(stats, lane, head, heads):
    wanted = (lane == head) | (lane == head + heads) | (lane == head + 2 * heads)
    return jnp.sum(jnp.where(wanted, stats, 0.0), axis=1, keepdims=True)


def head_columns(head):
    return pl.ds(pl.multiple_of(head * HEAD_DIM, HEAD_DIM), HEAD_DIM)


def mix_kernel(
    devices,
    n,
    chunk,
    start_ref,
    query_ref,
    key_ref,
    value_ref,
    weight_ref,
    out_ref,
    query_in,
    parts_own,
    parts_in,
    attended_ref,
    weights,
    away,
    near,
    landed,
    query_send,
    query_recv,
    parts_send,
    parts_recv,
    load_sem,
    send_sem,
    recv_sem,
):
    rows, width = out_ref.shape
    chunks = rows // chunk
    stages = n.bit_length() - 1
    hops = devices // 2
    heads = width // HEAD_DIM
    scale = HEAD_DIM ** (-0.5) * LOG2_E
    place = lax.axis_index("ctx")
    me = lax.axis_index("head")
    core = me % 2

    def flip(bit, by):
        return bit + by - 2 * bit * by

    def slot_bit(slot, stage):
        return (slot // (n >> (stage + 1))) % 2

    def destination(slot):
        to_core = flip(core, slot_bit(slot, 0))
        target = to_core
        for axis in range(1, stages):
            across = slot_bit(slot, axis) * (1 - to_core) + slot_bit(slot, stages - axis) * to_core
            target = target + flip((me // 2**axis) % 2, across) * 2**axis
        return target

    def partner(stage):
        if stage == 0:
            return me + 1 - 2 * core
        forward = me + (1 - 2 * ((me // 2**stage) % 2)) * 2**stage
        other = stages - stage
        backward = me + (1 - 2 * ((me // 2**other) % 2)) * 2**other
        return forward * (1 - core) + backward * core

    loads = []
    for slot in list(range(n // 2, n)) + list(range(n // 2)):
        columns = pl.ds(pl.multiple_of(destination(slot) * width, width), width)
        load = pltpu.make_async_copy(weight_ref.at[:, columns], weights.at[slot], load_sem.at[slot])
        load.start()
        loads.append((slot, load))

    barrier = pltpu.get_barrier_semaphore()
    for stage in range(stages):
        pl.semaphore_signal(barrier, inc=1, device_id={"head": partner(stage)}, device_id_type=MESH)

    @pl.when(place > 0)
    def _():
        pl.semaphore_signal(barrier, inc=1, device_id={"ctx": place - 1}, device_id_type=MESH)

    @pl.when(place < devices - 1)
    def _():
        pl.semaphore_signal(barrier, inc=1, device_id={"ctx": place + 1}, device_id_type=MESH)

    has_lower = (place + devices - 1) // devices
    has_upper = 1 - place // (devices - 1)
    pl.semaphore_wait(barrier, stages + has_lower + has_upper)

    def rows_of(part):
        return pl.ds(part * chunk, chunk)

    def query_copy(distance, part):
        source = query_ref if distance == 0 else query_in.at[distance - 1]
        return pltpu.make_async_remote_copy(
            src_ref=source.at[rows_of(part)],
            dst_ref=query_in.at[distance, rows_of(part)],
            send_sem=query_send.at[distance, part],
            recv_sem=query_recv.at[distance, part],
            device_id={"ctx": place - 1},
            device_id_type=MESH,
        )

    def parts_copy(distance, part):
        return pltpu.make_async_remote_copy(
            src_ref=parts_own.at[distance, rows_of(part)],
            dst_ref=parts_in.at[distance - 1, rows_of(part)],
            send_sem=parts_send.at[distance - 1, part],
            recv_sem=parts_recv.at[distance - 1, part],
            device_id={"ctx": place + 1},
            device_id_type=MESH,
        )

    def in_window(distance):
        return place + distance < devices

    def attend(distance, part):
        first = part * chunk if distance == hops else 0
        last = (part + 1) * chunk if distance == 0 else rows
        queries = query_ref if distance == 0 else query_in.at[distance - 1]
        lane = lax.broadcasted_iota(jnp.int32, (chunk, HEAD_DIM), 1)

        def one_head(head, stats):
            columns = head_columns(head)
            scores = lax.dot_general(
                queries[rows_of(part), columns],
                key_ref[first:last, columns],
                (((1,), (1,)), ((), ())),
                preferred_element_type=jnp.float32,
            )
            position = lax.broadcasted_iota(jnp.int32, scores.shape, 1) + (first - distance * rows)
            allowed = position >= start_ref[distance, rows_of(part), :]
            if distance == 0:
                allowed &= position <= lax.broadcasted_iota(jnp.int32, scores.shape, 0) + part * chunk
            scores = jnp.where(allowed, scores, -1e30)
            top = jnp.max(scores, axis=1, keepdims=True)
            probs = jnp.exp2((scores - top) * scale)
            total = jnp.sum(probs, axis=1, keepdims=True)
            weighted = dot32(probs.astype(jnp.bfloat16), value_ref[first:last, columns])
            parts_own[distance, rows_of(part), columns] = (weighted / total).astype(jnp.bfloat16)
            return spread_exactly(top * scale + jnp.log(total) * LOG2_E, lane, head, heads, stats)

        stats = lax.fori_loop(0, heads, one_head, jnp.zeros((chunk, HEAD_DIM), jnp.float32), unroll=2)
        parts_own[distance, rows_of(part), width:] = stats.astype(jnp.bfloat16)

    def merge(distance, part):
        lane = lax.broadcasted_iota(jnp.int32, (chunk, HEAD_DIM), 1)
        own_stats = parts_own[distance, rows_of(part), width:].astype(jnp.float32)
        in_stats = parts_in[distance, rows_of(part), width:].astype(jnp.float32)

        def one_head(head, stats):
            columns = head_columns(head)
            own, arrived = gathered(own_stats, lane, head, heads), gathered(in_stats, lane, head, heads)
            top = jnp.maximum(own, arrived)
            own_share, in_share = jnp.exp2(own - top), jnp.exp2(arrived - top)
            total = own_share + in_share
            merged = (
                parts_own[distance, rows_of(part), columns].astype(jnp.float32) * (own_share / total)
                + parts_in[distance, rows_of(part), columns].astype(jnp.float32) * (in_share / total)
            ).astype(jnp.bfloat16)
            if distance == 0:
                attended_ref[rows_of(part), columns] = merged
                return stats
            parts_own[distance, rows_of(part), columns] = merged
            return spread_exactly(top + jnp.log(total) * LOG2_E, lane, head, heads, stats)

        stats = lax.fori_loop(0, heads, one_head, jnp.zeros((chunk, HEAD_DIM), jnp.float32), unroll=2)
        if distance > 0:
            parts_own[distance, rows_of(part), width:] = stats.astype(jnp.bfloat16)

    def send_own_queries(part):
        @pl.when(place > 0)
        def _():
            query_copy(0, part).start()

    def near_distances(part):
        attend(0, part)
        for distance in range(1, hops):

            @pl.when(in_window(distance))
            def _():
                query_copy(distance - 1, part).wait_recv()

                @pl.when(place > 0)
                def _():
                    query_copy(distance, part).start()

        if part + 2 < chunks:
            send_own_queries(part + 2)
        for distance in range(1, hops):

            @pl.when(in_window(distance))
            def _():
                attend(distance, part)

                @pl.when(place == 0)
                def _():
                    parts_copy(distance, part).start()

    def far_distance(part):
        @pl.when(in_window(hops))
        def _():
            query_copy(hops - 1, part).wait_recv()
            attend(hops, part)
            parts_copy(hops, part).start()

    def merge_all(part):
        @pl.when(place > 0)
        def _():
            for distance in range(hops - 1, -1, -1):

                @pl.when(in_window(distance))
                def _():
                    parts_copy(distance + 1, part).wait_recv()
                    merge(distance, part)
                    if distance > 0:
                        parts_copy(distance, part).start()

        @pl.when(place == 0)
        def _():
            attended_ref[rows_of(part), :] = parts_own[0, rows_of(part), :width]

    first_of = [n - (n >> stage) for stage in range(stages)]

    def copy(stage, part):
        count = n >> (stage + 1)
        source = away.at[part] if stage == 0 else near.at[part, pl.ds(count, count)]
        return pltpu.make_async_remote_copy(
            src_ref=source,
            dst_ref=landed.at[part, pl.ds(first_of[stage], count)],
            send_sem=send_sem.at[stage, part],
            recv_sem=recv_sem.at[stage, part],
            device_id={"head": partner(stage)},
            device_id_type=MESH,
        )

    def term(part, slot):
        return jnp.dot(
            attended_ref[part * chunk : (part + 1) * chunk, :], weights[slot], preferred_element_type=jnp.float32
        )

    def far_terms(part):
        if part == 0:
            for _, load in loads[: n // 2]:
                load.wait()

        @pl.loop(0, n // 2)
        def _(index):
            away[part, index] = term(part, index + n // 2).astype(jnp.bfloat16)

        copy(0, part).start()

    def near_terms(part):
        if part == 0:
            for _, load in loads[n // 2 :]:
                load.wait()
        copy(0, part).wait_recv()

        def add(index):
            total = term(part, index) + landed[part, index].astype(jnp.float32)
            near[part, index] = total.astype(jnp.bfloat16)

        pl.loop(n // 4, n // 2)(add)
        copy(1, part).start()
        pl.loop(0, n // 4)(add)

    def fold(stage, part):
        copy(stage, part).wait_recv()
        half = n >> (stage + 2)

        def add(index):
            arrived = landed[part, first_of[stage] + index].astype(jnp.float32)
            near[part, index] = (near[part, index].astype(jnp.float32) + arrived).astype(jnp.bfloat16)

        pl.loop(half, 2 * half)(add)
        copy(stage + 1, part).start()
        pl.loop(0, half)(add)

    def finish(part):
        last = stages - 1
        copy(last, part).wait_recv()
        out_ref[part * chunk : (part + 1) * chunk, :] = near[part, 0].astype(jnp.float32) + landed[
            part, first_of[last]
        ].astype(jnp.float32)

    send_own_queries(0)
    if chunks > 1:
        send_own_queries(1)
    for step in range(chunks + stages + 2):
        if step < chunks:
            near_distances(step)
        if 0 <= step - 1 < chunks:
            far_distance(step - 1)
        if 0 <= step - 2 < chunks:
            merge_all(step - 2)
            far_terms(step - 2)
        for stage in range(1, stages):
            if 0 <= step - 2 - stage < chunks:
                near_terms(step - 3) if stage == 1 else fold(stage - 1, step - 2 - stage)
        if 0 <= step - 2 - stages < chunks:
            finish(step - 2 - stages)
    for part in range(chunks):
        for stage in range(stages):
            copy(stage, part).wait_send()
        for distance in range(hops):

            @pl.when((place > 0) & in_window(distance))
            def _():
                query_copy(distance, part).wait_send()

            @pl.when(in_window(distance + 1))
            def _():
                parts_copy(distance + 1, part).wait_send()


def mix(start, query, key, value, weight):
    rows, width = query.shape
    devices, n = lax.axis_size("ctx"), lax.axis_size("head")
    hops = devices // 2
    chunks = rows // MIX_ROWS
    stages = n.bit_length() - 1
    vmem = pl.BlockSpec(memory_space=pltpu.VMEM)
    return pl.pallas_call(
        functools.partial(mix_kernel, devices, n, MIX_ROWS),
        out_shape=jax.ShapeDtypeStruct((rows, width), jnp.float32),
        in_specs=[vmem] * 4 + [pl.BlockSpec(memory_space=pl.ANY)],
        out_specs=vmem,
        scratch_shapes=[
            pltpu.VMEM((hops, rows, width), jnp.bfloat16),
            pltpu.VMEM((hops + 1, rows, width + HEAD_DIM), jnp.bfloat16),
            pltpu.VMEM((hops, rows, width + HEAD_DIM), jnp.bfloat16),
            pltpu.VMEM((rows, width), jnp.bfloat16),
            pltpu.VMEM((n, width, width), jnp.bfloat16),
            pltpu.VMEM((chunks, n // 2, MIX_ROWS, width), jnp.bfloat16),
            pltpu.VMEM((chunks, n // 2, MIX_ROWS, width), jnp.bfloat16),
            pltpu.VMEM((chunks, n - 1, MIX_ROWS, width), jnp.bfloat16),
            pltpu.SemaphoreType.DMA((hops, chunks)),
            pltpu.SemaphoreType.DMA((hops, chunks)),
            pltpu.SemaphoreType.DMA((hops, chunks)),
            pltpu.SemaphoreType.DMA((hops, chunks)),
            pltpu.SemaphoreType.DMA((n,)),
            pltpu.SemaphoreType.DMA((stages, chunks)),
            pltpu.SemaphoreType.DMA((stages, chunks)),
        ],
        compiler_params=pltpu.CompilerParams(
            collective_id=0, has_side_effects=True, vmem_limit_bytes=60 * 2**20
        ),
        cost_estimate=pl.CostEstimate(flops=13 * 10**9, bytes_accessed=24 * 2**20, transcendentals=6 * 10**6),
    )(start, query, key, value, weight)


def on_device(
    hyena_query,
    hyena_key,
    hyena_value,
    hyena_filter,
    attn_query,
    attn_key,
    attn_value,
    segment_ids,
    out_weight,
):
    num_rows = hyena_key.shape[0]
    tap_count = hyena_filter.shape[0]
    hops = lax.axis_size("ctx") // 2
    last_key = hyena_key[num_rows - tap_count :].astype(jnp.float32)
    last_value = hyena_value[num_rows - tap_count :].astype(jnp.float32)
    rim = shifted((last_key * last_value).astype(jnp.bfloat16), "ctx", 1)
    devices = lax.axis_size("ctx")
    document_start = []
    for distance in range(hops + 1):
        offset = jnp.minimum(lax.axis_index("ctx") + distance, devices - 1) * num_rows
        segments = lax.dynamic_slice_in_dim(segment_ids, offset, num_rows)
        earlier = jnp.sum((segment_ids[None, :] < segments[:, None]).astype(jnp.int32), axis=1)
        document_start.append(earlier - offset)
    start = jnp.stack(document_start)[..., None]
    projected = mix(start, attn_query, attn_key, attn_value, out_weight)
    hyena_out, stream = hyena(rim, hyena_query, hyena_key, hyena_value, hyena_filter, projected)
    return (hyena_out, stream)


def solution(mesh):
    return jax.shard_map(
        on_device,
        mesh=mesh,
        in_specs=(
            P("ctx", "head"),
            P("ctx", "head"),
            P("ctx", "head"),
            P(None, "head"),
            P("ctx", "head"),
            P("ctx", "head"),
            P("ctx", "head"),
            P(),
            P("head", None),
        ),
        out_specs=(P("ctx", "head"), P("ctx", "head")),
        check_vma=False,
    )
```

```python
import functools

import jax
import jax.numpy as jnp
import numpy as np
from jax import lax
from jax.experimental import pallas as pl
from jax.experimental.pallas import tpu as pltpu
from jax.sharding import PartitionSpec as P

HEAD_DIM = 128
LOG2_E = 1.4426950408889634
CHANNEL_TILE = 256
MIX_ROWS = 128
MESH = pl.DeviceIdType.MESH


def shifted(x, axis, by):
    devices = lax.axis_size(axis)
    pairs = [(i, i + by) for i in range(devices) if 0 <= i + by < devices]
    return lax.ppermute(x, axis, pairs)


def split_high_low(matrix):
    exact = jnp.asarray(matrix, jnp.float32)
    high = exact.astype(jnp.bfloat16)
    low = (exact - high.astype(jnp.float32)).astype(jnp.bfloat16)
    return high, low


def fourier_matrices(taps):
    size = 2 * taps
    n = np.arange(size)
    k = np.arange(taps)
    angle = 2.0 * np.pi * np.outer(k, n) / size
    alternating = np.where(n % 2 == 0, 1.0, -1.0)
    forward = np.concatenate([np.cos(angle), alternating[None], np.sin(angle)[1:]], axis=0)
    gain = np.full((size,), 2.0 / size)
    gain[0] = gain[taps] = 1.0 / size
    inverse = (forward * gain[:, None]).T[taps:]
    return forward.astype(np.float32), inverse.astype(np.float32)


def dot32(a, b):
    return jnp.dot(a, b, preferred_element_type=jnp.float32)


def hyena_kernel(
    rim_ref, query_ref, key_ref, value_ref, taps_ref, projected_ref, fh_ref, fl_ref, gh_ref, gl_ref, out_ref, stream_ref
):
    rows, _ = key_ref.shape
    taps = taps_ref.shape[0]
    fh, fl, gh, gl = fh_ref[...], fl_ref[...], gh_ref[...], gl_ref[...]
    tap_freq = dot32(fh[:, :taps], taps_ref[...]) + dot32(fl[:, :taps], taps_ref[...])
    tap_cos, tap_sin = tap_freq[:taps], tap_freq[taps:]
    edge = lax.broadcasted_iota(jnp.int32, tap_cos.shape, 0) == 0
    before = rim_ref[...]
    for block in range(rows // taps):
        here = slice(block * taps, (block + 1) * taps)
        now = (key_ref[here, :].astype(jnp.float32) * value_ref[here, :].astype(jnp.float32)).astype(jnp.bfloat16)
        window = jnp.concatenate([before, now], axis=0)
        freq = dot32(fh, window) + dot32(fl, window)
        cos, sin = freq[:taps], freq[taps:]
        sin_sin = sin * tap_sin
        real = cos * tap_cos - jnp.where(edge, 0.0, sin_sin)
        imag = jnp.where(edge, sin_sin, cos * tap_sin + sin * tap_cos)
        product = jnp.concatenate([real, imag], axis=0)
        high = product.astype(jnp.bfloat16)
        low = (product - high.astype(jnp.float32)).astype(jnp.bfloat16)
        filtered = dot32(gh, high) + dot32(gh, low) + dot32(gl, high)
        hyena_out = (query_ref[here, :].astype(jnp.float32) * filtered).astype(jnp.bfloat16)
        out_ref[here, :] = hyena_out
        stream_ref[here, :] = (hyena_out.astype(jnp.float32) + projected_ref[here, :]).astype(jnp.bfloat16)
        before = now


def hyena(rim, query, key, value, taps, projected):
    rows, width = key.shape
    tap_count = taps.shape[0]
    forward, inverse = fourier_matrices(tap_count)
    constants = split_high_low(forward) + split_high_low(inverse)
    column = lambda r: pl.BlockSpec((r, CHANNEL_TILE), lambda i: (0, i))
    whole = lambda a: pl.BlockSpec(a.shape, lambda i: (0, 0))
    return pl.pallas_call(
        hyena_kernel,
        out_shape=[jax.ShapeDtypeStruct((rows, width), jnp.bfloat16)] * 2,
        grid=(width // CHANNEL_TILE,),
        in_specs=[column(tap_count), column(rows), column(rows), column(rows), column(tap_count), column(rows)]
        + [whole(a) for a in constants],
        out_specs=[column(rows)] * 2,
        compiler_params=pltpu.CompilerParams(vmem_limit_bytes=48 * 2**20),
        cost_estimate=pl.CostEstimate(flops=3 * 10**9, bytes_accessed=5 * 2**20, transcendentals=0),
    )(rim, query, key, value, taps, projected, *constants)


def spread_exactly(value, lane, head, heads, into):
    high = value.astype(jnp.bfloat16).astype(jnp.float32)
    middle = (value - high).astype(jnp.bfloat16).astype(jnp.float32)
    low = value - high - middle
    into = jnp.where(lane == head, high, into)
    into = jnp.where(lane == head + heads, middle, into)
    return jnp.where(lane == head + 2 * heads, low, into)


def gathered(stats, lane, head, heads):
    wanted = (lane == head) | (lane == head + heads) | (lane == head + 2 * heads)
    return jnp.sum(jnp.where(wanted, stats, 0.0), axis=1, keepdims=True)


def head_columns(head):
    return pl.ds(pl.multiple_of(head * HEAD_DIM, HEAD_DIM), HEAD_DIM)


def mix_kernel(
    devices,
    n,
    chunk,
    far_place,
    start_ref,
    query_ref,
    key_ref,
    value_ref,
    weight_ref,
    out_ref,
    query_in,
    parts_own,
    parts_in,
    attended_ref,
    weights,
    away,
    near,
    landed,
    query_send,
    query_recv,
    parts_send,
    parts_recv,
    load_sem,
    send_sem,
    recv_sem,
):
    rows, width = out_ref.shape
    chunks = rows // chunk
    stages = n.bit_length() - 1
    hops = devices // 2
    heads = width // HEAD_DIM
    scale = HEAD_DIM ** (-0.5) * LOG2_E
    place = lax.axis_index("ctx")
    me = lax.axis_index("head")
    core = me % 2

    def flip(bit, by):
        return bit + by - 2 * bit * by

    def slot_bit(slot, stage):
        return (slot // (n >> (stage + 1))) % 2

    def destination(slot):
        to_core = flip(core, slot_bit(slot, 0))
        target = to_core
        for axis in range(1, stages):
            across = slot_bit(slot, axis) * (1 - to_core) + slot_bit(slot, stages - axis) * to_core
            target = target + flip((me // 2**axis) % 2, across) * 2**axis
        return target

    def partner(stage):
        if stage == 0:
            return me + 1 - 2 * core
        forward = me + (1 - 2 * ((me // 2**stage) % 2)) * 2**stage
        other = stages - stage
        backward = me + (1 - 2 * ((me // 2**other) % 2)) * 2**other
        return forward * (1 - core) + backward * core

    loads = []
    for slot in list(range(n // 2, n)) + list(range(n // 2)):
        columns = pl.ds(pl.multiple_of(destination(slot) * width, width), width)
        load = pltpu.make_async_copy(weight_ref.at[:, columns], weights.at[slot], load_sem.at[slot])
        load.start()
        loads.append((slot, load))

    barrier = pltpu.get_barrier_semaphore()
    for stage in range(stages):
        pl.semaphore_signal(barrier, inc=1, device_id={"head": partner(stage)}, device_id_type=MESH)

    @pl.when(place > 0)
    def _():
        pl.semaphore_signal(barrier, inc=1, device_id={"ctx": place - 1}, device_id_type=MESH)

    @pl.when(place < devices - 1)
    def _():
        pl.semaphore_signal(barrier, inc=1, device_id={"ctx": place + 1}, device_id_type=MESH)

    has_lower = (place + devices - 1) // devices
    has_upper = 1 - place // (devices - 1)
    pl.semaphore_wait(barrier, stages + has_lower + has_upper)

    def rows_of(part):
        return pl.ds(part * chunk, chunk)

    def query_copy(distance, part):
        source = query_ref if distance == 0 else query_in.at[distance - 1]
        return pltpu.make_async_remote_copy(
            src_ref=source.at[rows_of(part)],
            dst_ref=query_in.at[distance, rows_of(part)],
            send_sem=query_send.at[distance, part],
            recv_sem=query_recv.at[distance, part],
            device_id={"ctx": place - 1},
            device_id_type=MESH,
        )

    def parts_copy(distance, part):
        return pltpu.make_async_remote_copy(
            src_ref=parts_own.at[distance, rows_of(part)],
            dst_ref=parts_in.at[distance - 1, rows_of(part)],
            send_sem=parts_send.at[distance - 1, part],
            recv_sem=parts_recv.at[distance - 1, part],
            device_id={"ctx": place + 1},
            device_id_type=MESH,
        )

    def in_window(distance):
        return place + distance < devices

    def reaches_below(distance):
        return place == far_place + 1 if distance == hops - 1 else (place > 0) & in_window(distance)

    def attend(distance, part):
        first = part * chunk if distance == hops else 0
        last = (part + 1) * chunk if distance == 0 else rows
        queries = query_ref if distance == 0 else query_in.at[distance - 1]
        lane = lax.broadcasted_iota(jnp.int32, (chunk, HEAD_DIM), 1)

        def one_head(head, stats):
            columns = head_columns(head)
            scores = lax.dot_general(
                queries[rows_of(part), columns],
                key_ref[first:last, columns],
                (((1,), (1,)), ((), ())),
                preferred_element_type=jnp.float32,
            )
            position = lax.broadcasted_iota(jnp.int32, scores.shape, 1) + (first - distance * rows)
            allowed = position >= start_ref[distance, rows_of(part), :]
            if distance == 0:
                allowed &= position <= lax.broadcasted_iota(jnp.int32, scores.shape, 0) + part * chunk
            scores = jnp.where(allowed, scores, -1e30)
            top = jnp.max(scores, axis=1, keepdims=True)
            probs = jnp.exp2((scores - top) * scale)
            total = jnp.sum(probs, axis=1, keepdims=True)
            weighted = dot32(probs.astype(jnp.bfloat16), value_ref[first:last, columns])
            parts_own[distance, rows_of(part), columns] = (weighted / total).astype(jnp.bfloat16)
            return spread_exactly(top * scale + jnp.log(total) * LOG2_E, lane, head, heads, stats)

        stats = lax.fori_loop(0, heads, one_head, jnp.zeros((chunk, HEAD_DIM), jnp.float32), unroll=2)
        parts_own[distance, rows_of(part), width:] = stats.astype(jnp.bfloat16)

    def merge(distance, part):
        lane = lax.broadcasted_iota(jnp.int32, (chunk, HEAD_DIM), 1)
        own_stats = parts_own[distance, rows_of(part), width:].astype(jnp.float32)
        in_stats = parts_in[distance, rows_of(part), width:].astype(jnp.float32)

        def one_head(head, stats):
            columns = head_columns(head)
            own, arrived = gathered(own_stats, lane, head, heads), gathered(in_stats, lane, head, heads)
            top = jnp.maximum(own, arrived)
            own_share, in_share = jnp.exp2(own - top), jnp.exp2(arrived - top)
            total = own_share + in_share
            merged = (
                parts_own[distance, rows_of(part), columns].astype(jnp.float32) * (own_share / total)
                + parts_in[distance, rows_of(part), columns].astype(jnp.float32) * (in_share / total)
            ).astype(jnp.bfloat16)
            if distance == 0:
                attended_ref[rows_of(part), columns] = merged
                return stats
            parts_own[distance, rows_of(part), columns] = merged
            return spread_exactly(top + jnp.log(total) * LOG2_E, lane, head, heads, stats)

        stats = lax.fori_loop(0, heads, one_head, jnp.zeros((chunk, HEAD_DIM), jnp.float32), unroll=2)
        if distance > 0:
            parts_own[distance, rows_of(part), width:] = stats.astype(jnp.bfloat16)

    def send_own_queries(part):
        @pl.when(place > 0)
        def _():
            query_copy(0, part).start()

    def near_distances(part):
        attend(0, part)
        for distance in range(1, hops):

            @pl.when(in_window(distance))
            def _():
                query_copy(distance - 1, part).wait_recv()

                @pl.when(reaches_below(distance))
                def _():
                    query_copy(distance, part).start()

        if part + 2 < chunks:
            send_own_queries(part + 2)
        for distance in range(1, hops):

            @pl.when(in_window(distance))
            def _():
                attend(distance, part)

                @pl.when(place != far_place + 1 if distance == hops - 1 else place == 0)
                def _():
                    parts_copy(distance, part).start()

    def far_distance(part):
        @pl.when(place == far_place)
        def _():
            query_copy(hops - 1, part).wait_recv()
            attend(hops, part)
            parts_copy(hops, part).start()

    def merge_all(part):
        for distance in range(hops - 1, -1, -1):

            @pl.when(reaches_below(distance))
            def _():
                parts_copy(distance + 1, part).wait_recv()
                merge(distance, part)
                if distance > 0:
                    parts_copy(distance, part).start()

        @pl.when(place == 0)
        def _():
            attended_ref[rows_of(part), :] = parts_own[0, rows_of(part), :width]

    first_of = [n - (n >> stage) for stage in range(stages)]

    def copy(stage, part):
        count = n >> (stage + 1)
        source = away.at[part] if stage == 0 else near.at[part, pl.ds(count, count)]
        return pltpu.make_async_remote_copy(
            src_ref=source,
            dst_ref=landed.at[part, pl.ds(first_of[stage], count)],
            send_sem=send_sem.at[stage, part],
            recv_sem=recv_sem.at[stage, part],
            device_id={"head": partner(stage)},
            device_id_type=MESH,
        )

    def term(part, slot):
        return jnp.dot(
            attended_ref[part * chunk : (part + 1) * chunk, :], weights[slot], preferred_element_type=jnp.float32
        )

    def far_terms(part):
        if part == 0:
            for _, load in loads[: n // 2]:
                load.wait()

        @pl.loop(0, n // 2)
        def _(index):
            away[part, index] = term(part, index + n // 2).astype(jnp.bfloat16)

        copy(0, part).start()

    def near_terms(part):
        if part == 0:
            for _, load in loads[n // 2 :]:
                load.wait()
        copy(0, part).wait_recv()

        def add(index):
            total = term(part, index) + landed[part, index].astype(jnp.float32)
            near[part, index] = total.astype(jnp.bfloat16)

        pl.loop(n // 4, n // 2)(add)
        copy(1, part).start()
        pl.loop(0, n // 4)(add)

    def fold(stage, part):
        copy(stage, part).wait_recv()
        half = n >> (stage + 2)

        def add(index):
            arrived = landed[part, first_of[stage] + index].astype(jnp.float32)
            near[part, index] = (near[part, index].astype(jnp.float32) + arrived).astype(jnp.bfloat16)

        pl.loop(half, 2 * half)(add)
        copy(stage + 1, part).start()
        pl.loop(0, half)(add)

    def finish(part):
        last = stages - 1
        copy(last, part).wait_recv()
        out_ref[part * chunk : (part + 1) * chunk, :] = near[part, 0].astype(jnp.float32) + landed[
            part, first_of[last]
        ].astype(jnp.float32)

    send_own_queries(0)
    if chunks > 1:
        send_own_queries(1)
    for step in range(chunks + stages + 2):
        if step < chunks:
            near_distances(step)
        if 0 <= step - 1 < chunks:
            far_distance(step - 1)
        if 0 <= step - 2 < chunks:
            merge_all(step - 2)
            far_terms(step - 2)
        for stage in range(1, stages):
            if 0 <= step - 2 - stage < chunks:
                near_terms(step - 3) if stage == 1 else fold(stage - 1, step - 2 - stage)
        if 0 <= step - 2 - stages < chunks:
            finish(step - 2 - stages)
    for part in range(chunks):
        for stage in range(stages):
            copy(stage, part).wait_send()
        for distance in range(hops):

            @pl.when(reaches_below(distance))
            def _():
                query_copy(distance, part).wait_send()

            @pl.when(place == far_place if distance == hops - 1 else in_window(distance + 1))
            def _():
                parts_copy(distance + 1, part).wait_send()


def mix(far_place, start, query, key, value, weight):
    rows, width = query.shape
    devices, n = lax.axis_size("ctx"), lax.axis_size("head")
    hops = devices // 2
    chunks = rows // MIX_ROWS
    stages = n.bit_length() - 1
    vmem = pl.BlockSpec(memory_space=pltpu.VMEM)
    return pl.pallas_call(
        functools.partial(mix_kernel, devices, n, MIX_ROWS, far_place),
        out_shape=jax.ShapeDtypeStruct((rows, width), jnp.float32),
        in_specs=[vmem] * 4 + [pl.BlockSpec(memory_space=pl.ANY)],
        out_specs=vmem,
        scratch_shapes=[
            pltpu.VMEM((hops, rows, width), jnp.bfloat16),
            pltpu.VMEM((hops + 1, rows, width + HEAD_DIM), jnp.bfloat16),
            pltpu.VMEM((hops, rows, width + HEAD_DIM), jnp.bfloat16),
            pltpu.VMEM((rows, width), jnp.bfloat16),
            pltpu.VMEM((n, width, width), jnp.bfloat16),
            pltpu.VMEM((chunks, n // 2, MIX_ROWS, width), jnp.bfloat16),
            pltpu.VMEM((chunks, n // 2, MIX_ROWS, width), jnp.bfloat16),
            pltpu.VMEM((chunks, n - 1, MIX_ROWS, width), jnp.bfloat16),
            pltpu.SemaphoreType.DMA((hops, chunks)),
            pltpu.SemaphoreType.DMA((hops, chunks)),
            pltpu.SemaphoreType.DMA((hops, chunks)),
            pltpu.SemaphoreType.DMA((hops, chunks)),
            pltpu.SemaphoreType.DMA((n,)),
            pltpu.SemaphoreType.DMA((stages, chunks)),
            pltpu.SemaphoreType.DMA((stages, chunks)),
        ],
        compiler_params=pltpu.CompilerParams(
            collective_id=far_place, has_side_effects=True, vmem_limit_bytes=60 * 2**20
        ),
        cost_estimate=pl.CostEstimate(flops=13 * 10**9, bytes_accessed=24 * 2**20, transcendentals=6 * 10**6),
    )(start, query, key, value, weight)


def on_device(
    hyena_query,
    hyena_key,
    hyena_value,
    hyena_filter,
    attn_query,
    attn_key,
    attn_value,
    segment_ids,
    out_weight,
):
    num_rows = hyena_key.shape[0]
    tap_count = hyena_filter.shape[0]
    hops = lax.axis_size("ctx") // 2
    last_key = hyena_key[num_rows - tap_count :].astype(jnp.float32)
    last_value = hyena_value[num_rows - tap_count :].astype(jnp.float32)
    rim = shifted((last_key * last_value).astype(jnp.bfloat16), "ctx", 1)
    devices = lax.axis_size("ctx")
    document_start = []
    for distance in range(hops + 1):
        offset = jnp.minimum(lax.axis_index("ctx") + distance, devices - 1) * num_rows
        segments = lax.dynamic_slice_in_dim(segment_ids, offset, num_rows)
        earlier = jnp.sum((segment_ids[None, :] < segments[:, None]).astype(jnp.int32), axis=1)
        document_start.append(earlier - offset)
    start = jnp.stack(document_start)[..., None]
    reaches = segment_ids[num_rows - 1 : hops * num_rows : num_rows] == segment_ids[hops * num_rows :: num_rows]
    far_place = jnp.sum(jnp.where(reaches, jnp.arange(hops, dtype=jnp.int32), 0))
    variants = [functools.partial(mix, at) for at in range(hops)]
    projected = lax.switch(far_place, variants, start, attn_query, attn_key, attn_value, out_weight)
    hyena_out, stream = hyena(rim, hyena_query, hyena_key, hyena_value, hyena_filter, projected)
    return (hyena_out, stream)


def solution(mesh):
    return jax.shard_map(
        on_device,
        mesh=mesh,
        in_specs=(
            P("ctx", "head"),
            P("ctx", "head"),
            P("ctx", "head"),
            P(None, "head"),
            P("ctx", "head"),
            P("ctx", "head"),
            P("ctx", "head"),
            P(),
            P("head", None),
        ),
        out_specs=(P("ctx", "head"), P("ctx", "head")),
        check_vma=False,
    )
```
